32 devices in a mesh: row: 8 (over y, x, core), col: 4 (over z).
Axes of the slice: x: 2, y: 2, z: 4, core: 2. Of those that a mesh axis runs over, the one named last changes fastest.
Arguments:
- window: float32 [8, 8192, 4, 1024], P('row', None, 'col'), may hold values from -7 to 8, as said below
Outputs:
- factored: float32 [8, 8192, 4, 1024], P('row', None, 'col')
The draws below stay inside these ranges and needn't reach their ends.
Inputs may be any that keep to these rules, and one draw needn't show every extreme that they name: `window`: entries above the diagonal are never read. The leading 2 * 128 by 256 block (lower triangle mirrored) is positive definite, with smallest eigenvalue 1 or more.
All inputs are finite; a program needn't handle non-finite values.
Results may differ from the reference program's by a relative error of at most 0.00028.
Values sent between devices are 32-bit elements; how exact they have to be, the bound alone decides.
No kernel may reach another device: no remote copies, remote signals or barrier semaphores. Data moves between devices by JAX's collectives and lax.ppermute only.
A program may use at most 192 MiB of HBM per device.

```python
import jax
import jax.numpy as jnp
from jax import lax

ORDER = 65536
NB = 128
WCOLS = 4096
N_ROW = 8
N_COL = 4


def draw_window(key, part):
    key_diag, key_place, key_values = jax.random.split(key, 3)
    shape = (ORDER, WCOLS)
    leading = 2 * NB
    row_ids = jnp.arange(ORDER)[:, None]
    col_ids = jnp.arange(WCOLS)[None, :]
    places = jax.random.uniform(key_place, (leading,), jnp.float32, 0.0, 1.0) * leading
    diag_add = jax.random.uniform(key_diag, (leading,), jnp.float32, 1.0, 2.0)
    row_place = places[jnp.minimum(jnp.arange(ORDER), leading - 1)][:, None]
    col_place = places[jnp.minimum(jnp.arange(WCOLS), leading - 1)][None, :]
    row_add = diag_add[jnp.minimum(jnp.arange(ORDER), leading - 1)][:, None]
    kernel = jnp.exp(-jnp.abs(row_place - col_place) / 3.0)
    inner = kernel + jnp.where(row_ids == col_ids, row_add, 0.0)
    values = jax.random.truncated_normal(key_values, -3.4, 3.4, shape, jnp.float32)
    outside = jnp.where(col_ids < leading, 0.5, 1.0) * values
    matrix = jnp.where((row_ids < leading) & (col_ids < leading), inner, outside)
    return matrix.reshape(ORDER // N_ROW, N_ROW, WCOLS // N_COL, N_COL).transpose(1, 0, 3, 2)


def setup_inputs(seed: int = 0) -> dict:
    arg_keys = jax.random.split(jax.random.key(seed), 2)
    return {
        "window": draw_window(jax.random.fold_in(arg_keys[1], 71), 0),
    }


def unpack(window):
    return window.transpose(1, 0, 3, 2).reshape(ORDER, WCOLS)

def pack(matrix):
    return matrix.reshape(ORDER // N_ROW, N_ROW, WCOLS // N_COL, N_COL).transpose(1, 0, 3, 2)

def reference(window):
    matrix = unpack(window)
    for panel_step in range(2):
        start = panel_step * NB
        finish = start + NB
        diag_tile = matrix[start:finish, start:finish]
        symmetric = jnp.tril(diag_tile) + jnp.tril(diag_tile, -1).T
        factor = jnp.tril(jnp.linalg.cholesky(symmetric))
        below = matrix[finish:, start:finish]
        solved = jax.scipy.linalg.solve_triangular(factor, below.T, lower=True).T
        panel = jnp.concatenate([jnp.zeros((start, NB), jnp.float32), factor, solved], 0)
        matrix = matrix.at[:, start:finish].set(panel)
        update = jnp.dot(panel, panel[finish:WCOLS].T, precision=lax.Precision.HIGHEST)
        matrix = matrix.at[:, finish:].add(-update)
    row_ids = jnp.arange(ORDER)[:, None]
    col_ids = jnp.arange(WCOLS)[None, :]
    matrix = jnp.where(row_ids >= col_ids, matrix, 0.0)
    return pack(matrix)
```

```python
import functools

import jax
import jax.numpy as jnp
from jax import lax
from jax.experimental import pallas as pl
from jax.experimental.pallas import tpu as pltpu
from jax.sharding import PartitionSpec as P

NB = 128
KW = 2 * NB
LANES = 128
BLOCK = 32
TILE = 512
F32 = jnp.float32
BF16 = jnp.bfloat16
HI = lax.Precision.HIGHEST
PARAMS = pltpu.CompilerParams(vmem_limit_bytes=48 * 1024 * 1024)


def iota(shape, dim):
    return lax.broadcasted_iota(jnp.int32, shape, dim)


def split(x):
    high = x.astype(BF16)
    return high, (x - high.astype(F32)).astype(BF16)


def dot3(a, b_high, b_low):
    a_high, a_low = split(a)
    dot = functools.partial(jnp.dot, preferred_element_type=F32)
    return dot(a_high, b_high) + (dot(a_high, b_low) + dot(a_low, b_high))


def pack_kernel(width, win_ref, out_ref):
    fold = LANES // width
    part = win_ref.shape[0] // fold
    tile = win_ref[:, 0, :]
    lane = iota((part, LANES), 1) // width
    out = tile[:part]
    for j in range(1, fold):
        rolled = pltpu.roll(tile[j * part : (j + 1) * part], j * width, 1)
        out = jnp.where(lane == j, rolled, out)
    out_ref[...] = out


def pack_rows(window, first, rows, tile, width):
    fold = LANES // width
    base = first // tile
    return pl.pallas_call(
        functools.partial(pack_kernel, width),
        grid=(rows // tile,),
        in_specs=[pl.BlockSpec((None, tile, 1, LANES), lambda i: (0, base + i, 0, 0))],
        out_specs=pl.BlockSpec((tile // fold, LANES), lambda i: (i, 0)),
        out_shape=jax.ShapeDtypeStruct((rows // fold, LANES), F32),
        compiler_params=PARAMS,
        name="pack",
    )(window)


def unpack(slots, width):
    fold = LANES // width
    part = slots[0].shape[0]
    lane = iota((part, LANES), 1) // width
    rows = []
    for j in range(fold):
        pieces = []
        for v in range(len(slots) // fold):
            piece = None
            for m in range(fold):
                slot = slots[v * fold + m]
                shift = (m - j) % fold
                moved = pltpu.roll(slot, shift * width, 1) if shift else slot
                piece = moved if piece is None else jnp.where(lane == m, moved, piece)
            pieces.append(piece)
        rows.append(jnp.concatenate(pieces, 1))
    return jnp.concatenate(rows, 0)


def slot_place(count, width, col_index):
    a = iota((KW, KW), 0)
    c = iota((KW, KW), 1)
    source = lax.rem(col_index - a // width + count, count)
    return (c == lax.rem(a, width) * count + source).astype(F32)


def interleave(ref, first, step, rows):
    for v in range(ref.shape[0]):
        piece = rows[:, v * LANES : (v + 1) * LANES]
        ref[v, pl.ds(first, rows.shape[0], stride=step), :] = piece


def whole_rows(ref):
    return jnp.concatenate([ref[v] for v in range(ref.shape[0])], 1)


def factor_kernel(
    count, width, place_ref, s_ref, high_ref, low_ref, diag_ref, z_ref, lt_ref, mix_ref
):
    row_count, height = s_ref.shape[0], s_ref.shape[1]
    for p in range(row_count):
        interleave(mix_ref, p, row_count, s_ref[p])
    place = slot_place(count, width, place_ref[1])
    s = jnp.dot(whole_rows(mix_ref), place, precision=HI, preferred_element_type=F32)
    r = iota((KW, KW), 0)
    c = iota((KW, KW), 1)
    z_ref[:, :KW] = jnp.where(r >= c, s, 0.0) + jnp.where(r > c, s, 0.0).T
    z_ref[:, KW:] = (r == c).astype(F32)
    rows = iota((BLOCK, 1), 0)
    for b in range(KW // BLOCK):
        top = b * BLOCK
        strip = z_ref[top : top + BLOCK, :]
        scale = jnp.zeros((BLOCK, 1), F32)
        for j in range(BLOCK):
            col = strip[:, top + j : top + j + 1]
            row = strip[j : j + 1, :]
            pivot = strip[j : j + 1, top + j : top + j + 1]
            ratio = jnp.where(rows > j, col / pivot, 0.0)
            scale = jnp.where(rows == j, lax.rsqrt(pivot), scale)
            strip = strip - ratio * row
        strip = strip * scale
        z_ref[top : top + BLOCK, :] = strip
        lt_ref[top : top + BLOCK, :] = strip[:, :KW]
        if top + BLOCK < KW:
            update = lax.dot_general(
                strip[:, :KW], strip, (((0,), (0,)), ((), ())), precision=HI,
                preferred_element_type=F32,
            )
            z_ref[top + BLOCK :, :] = z_ref[top + BLOCK :, :] - update[top + BLOCK :, :]
    contract_last = (((1,), (1,)), ((), ()))
    inverse = z_ref[:, KW:]
    inverse = jnp.where(r >= c, inverse, 0.0)
    weights = lax.dot_general(
        place, inverse, contract_last, precision=HI, preferred_element_type=F32
    )
    high_ref[...], low_ref[...] = split(weights)
    upper = jnp.where(r <= c, lt_ref[...], 0.0)
    pick = iota((height, KW), 1) == iota((height, KW), 0) * row_count + place_ref[0]
    diag_ref[...] = lax.dot_general(
        pick.astype(F32), upper, contract_last, precision=HI, preferred_element_type=F32
    )


def factor_call(place, gathered, count, width):
    row_count, height = gathered.shape[0], gathered.shape[1]
    whole = lambda *shape: pl.BlockSpec(shape, lambda i, place: (0,) * len(shape))
    return pl.pallas_call(
        functools.partial(factor_kernel, count, width),
        grid_spec=pltpu.PrefetchScalarGridSpec(
            num_scalar_prefetch=1,
            grid=(1,),
            in_specs=[whole(row_count, height, KW)],
            out_specs=[whole(KW, KW), whole(KW, KW), whole(height, KW)],
            scratch_shapes=[
                pltpu.VMEM((KW, 2 * KW), F32),
                pltpu.VMEM((KW, KW), F32),
                pltpu.VMEM((KW // LANES, KW, LANES), F32),
            ],
        ),
        out_shape=[
            jax.ShapeDtypeStruct((KW, KW), BF16),
            jax.ShapeDtypeStruct((KW, KW), BF16),
            jax.ShapeDtypeStruct((height, KW), F32),
        ],
        compiler_params=PARAMS,
        name="factor",
    )(place, gathered)


def columns_kernel(count, width, place_ref, head_ref, nh_ref, nl_ref, high_ref, low_ref, scr_ref):
    groups = head_ref.shape[0]
    tiles = head_ref.shape[1]
    height = head_ref.shape[3] * (LANES // width)
    for a in range(groups):
        for t in range(tiles):
            raw = unpack([head_ref[a, t, s] for s in range(count)], width)
            panel = dot3(raw, nh_ref[...], nl_ref[...])
            interleave(scr_ref, t * height * groups + a, groups, panel)
    cols = scr_ref.shape[1]
    l = iota((cols, KW), 0)
    c = iota((cols, KW), 1)
    pick = jnp.where(c == l * count + place_ref[1], -1.0, 0.0)
    weights = jnp.where(l < width, pick, whole_rows(scr_ref)).T
    high_ref[...], low_ref[...] = split(weights)


def columns_call(place, head, n_high, n_low, count, width, cols):
    whole = lambda *shape: pl.BlockSpec(shape, lambda i, place: (0,) * len(shape))
    return pl.pallas_call(
        functools.partial(columns_kernel, count, width),
        grid_spec=pltpu.PrefetchScalarGridSpec(
            num_scalar_prefetch=1,
            grid=(1,),
            in_specs=[whole(*head.shape), whole(KW, KW), whole(KW, KW)],
            out_specs=[whole(KW, cols), whole(KW, cols)],
            scratch_shapes=[pltpu.VMEM((KW // LANES, cols, LANES), F32)],
        ),
        out_shape=[jax.ShapeDtypeStruct((KW, cols), BF16)] * 2,
        compiler_params=PARAMS,
        name="columns",
    )(place, head, n_high, n_low)


def update_kernel(count, width, row_count, head, aliased, place_ref, *refs):
    slots_in = refs[: 2 * count - 1]
    nh_ref, nl_ref, wh_ref, wl_ref, diag_ref, win_ref = refs[2 * count - 1 : 2 * count + 5]
    out_ref = refs[-1]
    p, q = place_ref[0], place_ref[1]
    slots = [slots_in[0][...]]
    for s in range(1, count):
        slots.append(jnp.where(q >= s, slots_in[s][...], slots_in[2 * count - 1 - s][...]))
    panel = dot3(unpack(slots, width), nh_ref[...], nl_ref[...])
    tile = panel.shape[0]
    lane = iota((tile, LANES), 1)
    row = iota((tile, LANES), 0)
    if head:
        height = diag_ref.shape[0]
        first = pl.program_id(0) == 0
        top = jnp.where(first, diag_ref[...], panel[:height])
        panel = jnp.concatenate([top, panel[height:]], 0)
        global_row = (row + pl.program_id(0) * tile) * row_count + p
    high, low = split(panel)
    dot = functools.partial(jnp.dot, preferred_element_type=F32)
    groups = wh_ref.shape[1] // LANES
    for pair in range(groups // 2):
        span = slice(pair * 2 * LANES, (pair + 1) * 2 * LANES)
        w_high, w_low = wh_ref[:, span], wl_ref[:, span]
        update = dot(high, w_high) + (dot(high, w_low) + dot(low, w_high))
        for half in range(2):
            g = pair * 2 + half
            old = win_ref[pl.ds(g, tile, stride=groups), :]
            if g * LANES < width:
                old = jnp.where(lane < width - g * LANES, 0.0, old)
            new = old - update[:, half * LANES : (half + 1) * LANES]
            if head:
                global_col = (lane + g * LANES) * count + q
                new = jnp.where(global_row >= global_col, new, 0.0)
            out_ref[pl.ds(g, tile, stride=groups), :] = new


def update_call(place, chunk, weights, flat, out, first, rows, tile, count, width, row_count):
    fold = LANES // width
    groups = weights[2].shape[1] // LANES
    base = first // tile
    whole = lambda x: pl.BlockSpec(x.shape, lambda i, place: (0,) * x.ndim)
    part = (tile // fold, LANES)
    specs = [pl.BlockSpec(part, lambda i, place: (i, 0))]
    for s in range(1, count):
        index = lambda i, place, s=s: (jnp.where(place[1] >= s, i, 0), 0)
        specs.append(pl.BlockSpec(part, index))
    for s in range(1, count):
        index = lambda i, place, s=s: (jnp.where(place[1] < count - s, i, 0), 0)
        specs.append(pl.BlockSpec(part, index))
    wide = pl.BlockSpec((tile * groups, LANES), lambda i, place: (base + i, 0))
    specs += [whole(x) for x in weights] + [wide]
    operands = [*chunk, *weights, flat]
    aliases = {}
    if out is not None:
        specs.append(pl.BlockSpec(memory_space=pl.ANY))
        operands.append(out)
        aliases = {len(operands): 0}
    kernel = functools.partial(
        update_kernel, count, width, row_count, first == 0, out is not None
    )
    return pl.pallas_call(
        kernel,
        grid_spec=pltpu.PrefetchScalarGridSpec(
            num_scalar_prefetch=1,
            grid=(rows // tile,),
            in_specs=specs,
            out_specs=wide,
        ),
        out_shape=jax.ShapeDtypeStruct(flat.shape, F32),
        input_output_aliases=aliases,
        compiler_params=PARAMS,
        cost_estimate=pl.CostEstimate(
            flops=6 * rows * KW * (KW + groups * LANES),
            bytes_accessed=rows * 4 * (2 * groups * LANES + KW),
            transcendentals=0,
        ),
        name="update",
    )(place, *operands)


def chunk_sizes(rest, tile):
    units = rest // tile
    sizes = []
    for share in (3, 3, 3):
        take = min(units, max(1, -(-rest // tile * share // 10)))
        if take:
            sizes.append(take * tile)
        units -= take
    if units:
        sizes.append(units * tile)
    return sizes


def body(window):
    local_rows = window.shape[1]
    local_cols = window.shape[3]
    row_count = lax.axis_size("row")
    count = lax.axis_size("col")
    p = lax.axis_index("row")
    q = lax.axis_index("col")
    width = KW // count
    height = KW // row_count
    head_rows = local_cols * count // row_count
    groups = row_count // count
    tile = min(TILE, head_rows)
    place = jnp.stack([p, q]).astype(jnp.int32)
    flat = window.reshape(local_rows * local_cols // LANES, LANES)

    sizes = [head_rows] + chunk_sizes(local_rows - head_rows, tile)
    starts = [sum(sizes[:i]) for i in range(len(sizes))]
    packed = [pack_rows(window, f, r, tile, width) for f, r in zip(starts, sizes)]

    ups = [[x] for x in packed]
    downs = [[x] for x in packed]

    def hop(j, s):
        up = [(i, i + 1) for i in range(s, count - 1)]
        down = [(i + 1, i) for i in range(count - 1 - s)]
        ups[j].append(lax.ppermute(ups[j][-1], "col", up))
        downs[j].append(lax.ppermute(downs[j][-1], "col", down))

    for s in range(count - 1):
        hop(0, s)
    for s in range(count - 1):
        for j in range(1, len(sizes)):
            hop(j, s)

    mine = [packed[0]]
    for s in range(1, count):
        mine.append(jnp.where(q >= s, ups[0][s], downs[0][count - s]))
    mine = jnp.stack(mine)

    lead = mine[:, : tile // (LANES // width)][:, :height, :width]
    lead = lead.transpose(1, 0, 2).reshape(height, KW)
    gathered = lax.all_gather(lead, "row")
    n_high, n_low, diag = factor_call(place, gathered, count, width)

    spread = mine
    bit = 1
    while bit < count:
        pairs = [(i, i ^ bit) for i in range(row_count)]
        other = lax.ppermute(spread, "row", pairs)
        spread = jnp.where(((p ^ q) & bit) != 0, other, spread)
        bit *= 2
    spread = spread[None]
    while bit < row_count:
        pairs = [(i, i ^ bit) for i in range(row_count)]
        other = lax.ppermute(spread, "row", pairs)
        low = (p & bit) == 0
        spread = jnp.concatenate(
            [jnp.where(low, spread, other), jnp.where(low, other, spread)], 0
        )
        bit *= 2
    fold = LANES // width
    spread = spread.reshape(groups, count, head_rows // tile, tile // fold, LANES)
    spread = spread.transpose(0, 2, 1, 3, 4)
    w_high, w_low = columns_call(place, spread, n_high, n_low, count, width, local_cols)

    weights = [n_high, n_low, w_high, w_low, diag]
    out = None
    for j, (first, rows) in enumerate(zip(starts, sizes)):
        chunk = [packed[j]] + ups[j][1:] + downs[j][1:]
        out = update_call(
            place, chunk, weights, flat, out, first, rows, tile, count, width, row_count
        )
    return out.reshape(window.shape)


def solution(mesh):
    spec = P("row", None, "col", None)
    return jax.shard_map(body, mesh=mesh, in_specs=(spec,), out_specs=spec, check_vma=False)
```

```python
import functools

import jax
import jax.numpy as jnp
from jax import lax
from jax.experimental import pallas as pl
from jax.experimental.pallas import tpu as pltpu
from jax.sharding import PartitionSpec as P

NB = 128
KW = 2 * NB
LANES = 128
BLOCK = 32
TILE = 512
SHARES = (9, 4)
DEPTH = 6
F32 = jnp.float32
BF16 = jnp.bfloat16
HI = lax.Precision.HIGHEST
PARAMS = pltpu.CompilerParams(vmem_limit_bytes=32 * 1024 * 1024)

LIGHT = pl.CostEstimate(flops=0, bytes_accessed=0, transcendentals=0)


def iota(shape, dim):
    return lax.broadcasted_iota(jnp.int32, shape, dim)


def split(x):
    high = x.astype(BF16)
    return high, (x - high.astype(F32)).astype(BF16)


def dot3(a, b_high, b_low):
    a_high, a_low = split(a)
    dot = functools.partial(jnp.dot, preferred_element_type=F32)
    return dot(a_high, b_high) + (dot(a_high, b_low) + dot(a_low, b_high))


def pack_kernel(width, win_ref, out_ref):
    fold = LANES // width
    part = win_ref.shape[0] // fold
    tile = win_ref[:, 0, :]
    lane = iota((part, LANES), 1) // width
    out = tile[:part]
    for j in range(1, fold):
        rolled = pltpu.roll(tile[j * part : (j + 1) * part], j * width, 1)
        out = jnp.where(lane == j, rolled, out)
    out_ref[...] = out


def pack_rows(window, first, rows, tile, width):
    fold = LANES // width
    base = first // tile
    return pl.pallas_call(
        functools.partial(pack_kernel, width),
        grid=(rows // tile,),
        in_specs=[pl.BlockSpec((None, tile, 1, LANES), lambda i: (0, base + i, 0, 0))],
        out_specs=pl.BlockSpec((tile // fold, LANES), lambda i: (i, 0)),
        out_shape=jax.ShapeDtypeStruct((rows // fold, LANES), F32),
        compiler_params=PARAMS,
        cost_estimate=LIGHT,
        name="pack",
    )(window)


def unpack(slots, width):
    fold = LANES // width
    part = slots[0].shape[0]
    lane = iota((part, LANES), 1) // width
    rows = []
    for j in range(fold):
        pieces = []
        for v in range(len(slots) // fold):
            piece = None
            for m in range(fold):
                slot = slots[v * fold + m]
                shift = (m - j) % fold
                moved = pltpu.roll(slot, shift * width, 1) if shift else slot
                piece = moved if piece is None else jnp.where(lane == m, moved, piece)
            pieces.append(piece)
        rows.append(jnp.concatenate(pieces, 1))
    return jnp.concatenate(rows, 0)


def slot_place(count, width, col_index):
    a = iota((KW, KW), 0)
    c = iota((KW, KW), 1)
    source = lax.rem(col_index - a // width + count, count)
    return (c == lax.rem(a, width) * count + source).astype(F32)


def interleave(ref, first, step, rows):
    for v in range(ref.shape[0]):
        piece = rows[:, v * LANES : (v + 1) * LANES]
        ref[v, pl.ds(first, rows.shape[0], stride=step), :] = piece


def whole_rows(ref):
    return jnp.concatenate([ref[v] for v in range(ref.shape[0])], 1)


def eliminate(z_ref, lt_ref):
    rows = iota((BLOCK, 1), 0)
    for b in range(KW // BLOCK):
        top = b * BLOCK
        strip = z_ref[top : top + BLOCK, :]
        scale = jnp.zeros((BLOCK, 1), F32)
        for j in range(BLOCK):
            col = strip[:, top + j : top + j + 1]
            row = strip[j : j + 1, :]
            pivot = strip[j : j + 1, top + j : top + j + 1]
            ratio = jnp.where(rows > j, col / pivot, 0.0)
            scale = jnp.where(rows == j, lax.rsqrt(pivot), scale)
            strip = strip - ratio * row
        strip = strip * scale
        z_ref[top : top + BLOCK, :] = strip
        lt_ref[top : top + BLOCK, :] = strip[:, :KW]
        if top + BLOCK < KW:
            update = lax.dot_general(
                strip[:, :KW], strip, (((0,), (0,)), ((), ())), precision=HI,
                preferred_element_type=F32,
            )
            z_ref[top + BLOCK :, :] = z_ref[top + BLOCK :, :] - update[top + BLOCK :, :]


def factor_kernel(
    count, width, place_ref, s_ref, high_ref, low_ref, diag_ref, z_ref, lt_ref, mix_ref
):
    row_count, height = s_ref.shape[0], s_ref.shape[1]
    for p in range(row_count):
        interleave(mix_ref, p, row_count, s_ref[p])
    place = slot_place(count, width, place_ref[1])
    s = jnp.dot(whole_rows(mix_ref), place, precision=HI, preferred_element_type=F32)
    r = iota((KW, KW), 0)
    c = iota((KW, KW), 1)
    z_ref[:, :KW] = jnp.where(r >= c, s, 0.0) + jnp.where(r > c, s, 0.0).T
    z_ref[:, KW:] = (r == c).astype(F32)
    eliminate(z_ref, lt_ref)
    contract_last = (((1,), (1,)), ((), ()))
    inverse = jnp.where(r >= c, z_ref[:, KW:], 0.0)
    weights = lax.dot_general(
        place, inverse, contract_last, precision=HI, preferred_element_type=F32
    )
    high_ref[...], low_ref[...] = split(weights)
    upper = jnp.where(r <= c, lt_ref[...], 0.0)
    pick = iota((height, KW), 1) == iota((height, KW), 0) * row_count + place_ref[0]
    diag_ref[...] = lax.dot_general(
        pick.astype(F32), upper, contract_last, precision=HI, preferred_element_type=F32
    )


def whole(*shape):
    return pl.BlockSpec(shape, lambda i, place: (0,) * len(shape))


def factor_call(place, gathered, count, width):
    row_count, height = gathered.shape[0], gathered.shape[1]
    return pl.pallas_call(
        functools.partial(factor_kernel, count, width),
        grid_spec=pltpu.PrefetchScalarGridSpec(
            num_scalar_prefetch=1,
            grid=(1,),
            in_specs=[whole(row_count, height, KW)],
            out_specs=[whole(KW, KW), whole(KW, KW), whole(height, KW)],
            scratch_shapes=[
                pltpu.VMEM((KW, 2 * KW), F32),
                pltpu.VMEM((KW, KW), F32),
                pltpu.VMEM((KW // LANES, KW, LANES), F32),
            ],
        ),
        out_shape=[
            jax.ShapeDtypeStruct((KW, KW), BF16),
            jax.ShapeDtypeStruct((KW, KW), BF16),
            jax.ShapeDtypeStruct((height, KW), F32),
        ],
        compiler_params=PARAMS,
        cost_estimate=LIGHT,
        name="factor",
    )(place, gathered)


def columns_kernel(count, width, place_ref, head_ref, nh_ref, nl_ref, high_ref, low_ref, scr_ref):
    groups = head_ref.shape[0]
    tiles = head_ref.shape[2]
    height = head_ref.shape[3] * (LANES // width)
    for a in range(groups):
        for t in range(tiles):
            raw = unpack([head_ref[a, s, t] for s in range(count)], width)
            panel = dot3(raw, nh_ref[...], nl_ref[...])
            interleave(scr_ref, t * height * groups + a, groups, panel)
    cols = scr_ref.shape[1]
    l = iota((cols, KW), 0)
    c = iota((cols, KW), 1)
    pick = jnp.where(c == l * count + place_ref[1], -1.0, 0.0)
    weights = jnp.where(l < width, pick, whole_rows(scr_ref)).T
    high_ref[...], low_ref[...] = split(weights)


def columns_call(place, head, n_high, n_low, count, width, cols):
    return pl.pallas_call(
        functools.partial(columns_kernel, count, width),
        grid_spec=pltpu.PrefetchScalarGridSpec(
            num_scalar_prefetch=1,
            grid=(1,),
            in_specs=[whole(*head.shape), whole(KW, KW), whole(KW, KW)],
            out_specs=[whole(KW, cols), whole(KW, cols)],
            scratch_shapes=[pltpu.VMEM((KW // LANES, cols, LANES), F32)],
        ),
        out_shape=[jax.ShapeDtypeStruct((KW, cols), BF16)] * 2,
        compiler_params=PARAMS,
        cost_estimate=LIGHT,
        name="columns",
    )(place, head, n_high, n_low)


def update_kernel(count, width, row_count, first, skip, rows, tile, place_ref, *refs):
    ins = len(refs) - 10 - (first > 0)
    slots_in = refs[:ins]
    nh_ref, nl_ref, wh_ref, wl_ref, diag_ref, win_ref = refs[ins : ins + 6]
    out_ref, ring_ref, in_sem, out_sem = refs[-4:]
    p, q = place_ref[0], place_ref[1]
    groups = wh_ref.shape[1] // LANES
    part = tile // (LANES // width)
    steps = rows // tile
    depth = ring_ref.shape[0]
    ahead = steps if steps <= depth else depth // 2
    height = tile * groups
    dot = functools.partial(jnp.dot, preferred_element_type=F32)

    def place_of(i):
        return pl.ds(pl.multiple_of(first * groups + i * height, height), height)

    def fetch(i):
        slot = lax.rem(i, depth)
        return pltpu.make_async_copy(win_ref.at[place_of(i), :], ring_ref.at[slot], in_sem.at[slot])

    def store(i):
        slot = lax.rem(i, depth)
        return pltpu.make_async_copy(ring_ref.at[slot], out_ref.at[place_of(i), :], out_sem.at[slot])

    for i in range(ahead):
        fetch(jnp.int32(i)).start()

    def step(i, carry):
        span = pl.ds(pl.multiple_of(skip // (LANES // width) + i * part, part), part)
        slots = [slots_in[s][span, :] for s in range(count)]
        if ins > count:
            forwarded = slots_in[count][span, :]
            slots[1] = jnp.where(q == 0, forwarded, slots[1])
            slots[count - 1] = jnp.where(q == count - 1, forwarded, slots[count - 1])
        panel = dot3(unpack(slots, width), nh_ref[...], nl_ref[...])
        lane = iota((tile, LANES), 1)
        if first == 0:
            tall = diag_ref.shape[0]
            top = jnp.where(i == 0, diag_ref[...], panel[:tall])
            panel = jnp.concatenate([top, panel[tall:]], 0)
            global_row = (iota((tile, LANES), 0) + i * tile) * row_count + p
        high, low = split(panel)
        fetch(i).wait()
        buf = ring_ref.at[lax.rem(i, depth)]
        for pair in range(groups // 2):
            cols = slice(pair * 2 * LANES, (pair + 1) * 2 * LANES)
            w_high, w_low = wh_ref[:, cols], wl_ref[:, cols]
            update = dot(high, w_high) + (dot(high, w_low) + dot(low, w_high))
            for half in range(2):
                g = pair * 2 + half
                old = buf[pl.ds(g, tile, stride=groups), :]
                if g * LANES < width:
                    old = jnp.where(lane < width - g * LANES, 0.0, old)
                new = old - update[:, half * LANES : (half + 1) * LANES]
                if first == 0:
                    global_col = (lane + g * LANES) * count + q
                    new = jnp.where(global_row >= global_col, new, 0.0)
                buf[pl.ds(g, tile, stride=groups), :] = new
        store(i).start()

        @pl.when(i + ahead < steps)
        def _():
            @pl.when(i + ahead >= depth)
            def _():
                store(i + ahead - depth).wait()

            fetch(i + ahead).start()

        return carry

    lax.fori_loop(0, steps, step, 0)

    def drain(i, carry):
        store(i).wait()
        return carry

    lax.fori_loop(max(0, steps - depth), steps, drain, 0)


def update_call(
    place, chunk, weights, flat, out, first, skip, rows, tile, count, width, row_count
):
    groups = weights[2].shape[1] // LANES
    held = pl.BlockSpec(memory_space=pltpu.VMEM)
    far = pl.BlockSpec(memory_space=pl.ANY)
    specs = [held] * (len(chunk) + len(weights)) + [far]
    operands = [*chunk, *weights, flat]
    aliases = {}
    if out is not None:
        specs.append(far)
        operands.append(out)
        aliases = {len(operands): 0}
    depth = min(DEPTH, rows // tile)
    return pl.pallas_call(
        functools.partial(update_kernel, count, width, row_count, first, skip, rows, tile),
        grid_spec=pltpu.PrefetchScalarGridSpec(
            num_scalar_prefetch=1,
            grid=(1,),
            in_specs=specs,
            out_specs=far,
            scratch_shapes=[
                pltpu.VMEM((depth, tile * groups, LANES), F32),
                pltpu.SemaphoreType.DMA((depth,)),
                pltpu.SemaphoreType.DMA((depth,)),
            ],
        ),
        out_shape=jax.ShapeDtypeStruct(flat.shape, F32),
        input_output_aliases=aliases,
        compiler_params=PARAMS,
        cost_estimate=pl.CostEstimate(
            flops=6 * rows * KW * (KW + groups * LANES),
            bytes_accessed=rows * 4 * (2 * groups * LANES + KW),
            transcendentals=0,
        ),
        name="update",
    )(place, *operands)


def chunk_sizes(units):
    sizes = [1]
    for share in SHARES:
        sizes.append(max(1, units * share // 16))
    return sizes + [units - sum(sizes)]


def body(window):
    local_rows = window.shape[1]
    local_cols = window.shape[3]
    row_count = lax.axis_size("row")
    count = lax.axis_size("col")
    p = lax.axis_index("row")
    q = lax.axis_index("col")
    width = KW // count
    height = KW // row_count
    head_rows = local_cols * count // row_count
    groups = row_count // count
    tile = min(TILE, head_rows)
    place = jnp.stack([p, q]).astype(jnp.int32)
    flat = window.reshape(local_rows * local_cols // LANES, LANES)

    sizes = [x * tile for x in chunk_sizes(local_rows // tile)]
    starts = [sum(sizes[:i]) for i in range(len(sizes))]
    packed = [pack_rows(window, f, r, tile, width) for f, r in zip(starts, sizes)]

    def shift(x, k):
        return lax.ppermute(x, "col", [(i, (i + k) % count) for i in range(count)])

    fold = LANES // width
    slots = [[packed[0]] + [shift(packed[0], k) for k in range(1, count)]]
    early = tuple(packed[1:3])
    slots[0] = list(lax.optimization_barrier((*slots[0], *early)))[:count]
    head = jnp.stack(slots[0])

    lead = head[:, :height, :width]
    lead = lead.transpose(1, 0, 2).reshape(height, KW)
    gathered = lax.all_gather(lead, "row")
    n_high, n_low, diag = factor_call(place, gathered, count, width)

    spread = head
    bit = 1
    while bit < count:
        pairs = [(i, i ^ bit) for i in range(row_count)]
        other = lax.ppermute(spread, "row", pairs)
        spread = jnp.where(((p ^ q) & bit) != 0, other, spread)
        bit *= 2
    spread = spread[None]
    while bit < row_count:
        pairs = [(i, i ^ bit) for i in range(row_count)]
        other = lax.ppermute(spread, "row", pairs)
        low = (p & bit) == 0
        spread = jnp.concatenate(
            [jnp.where(low, spread, other), jnp.where(low, other, spread)], 0
        )
        bit *= 2
    spread = spread.reshape(groups, count, head_rows // tile, tile // fold, LANES)

    def update(j, out, skip=0, rows=None):
        rows = sizes[j] - skip if rows is None else rows
        return update_call(
            place, slots[j], weights, flat, out, starts[j] + skip, skip, rows, tile,
            count, width, row_count,
        )

    after = lambda x, *others: lax.optimization_barrier((x, *others))[0]

    if count != 4:
        slots += [[x] + [shift(x, k) for k in range(1, count)] for x in packed[1:]]
        made = columns_call(place, spread, n_high, n_low, count, width, local_cols)
        weights = [n_high, n_low, *made, diag]
        out = None
        for j in range(len(sizes)):
            out = update(j, out)
        return out.reshape(window.shape)

    up = [(0, 1), (1, 2), (2, 3)]
    down = [(1, 0), (2, 1), (3, 2)]
    outward = [(2, 3), (1, 0)]
    send = lambda x, pairs: lax.ppermute(x, "col", pairs)

    def forward(j, *others):
        slots[j].append(send(after(slots[j][2], *others), outward))

    x = packed[1]
    slots.append([x, send(x, up), shift(x, 2), send(x, down)])
    two = shift(packed[2], 2)
    forward(1, n_high)
    made = columns_call(place, spread, n_high, n_low, count, width, local_cols)
    weights = [n_high, n_low, *made, diag]
    out = update(0, None)
    x, third, out, *_ = lax.optimization_barrier(
        (packed[2], packed[3], out, slots[1][1], slots[1][3])
    )
    slots.append([x, send(x, up), two, send(x, down)])
    part = -(-sizes[1] // tile // 2) * tile
    out = update(1, out, rows=part)
    slots[2][2], third, out = lax.optimization_barrier((slots[2][2], third, out))
    forward(2)
    slots.append([third, send(third, up), shift(third, 2), send(third, down)])
    out = update(1, out, skip=part)
    slots[3][2], out = lax.optimization_barrier((slots[3][2], out))
    forward(3)
    out = update(2, out)
    out = update(3, out)
    return out.reshape(window.shape)


def solution(mesh):
    spec = P("row", None, "col", None)
    return jax.shard_map(body, mesh=mesh, in_specs=(spec,), out_specs=spec, check_vma=False)
```

```python
import functools

import jax
import jax.numpy as jnp
from jax import lax
from jax.experimental import pallas as pl
from jax.experimental.pallas import tpu as pltpu
from jax.sharding import PartitionSpec as P

NB = 128
KW = 2 * NB
LANES = 128
BLOCK = 32
TILE = 512
SHARES = (9, 4)
DEPTH = 6
F32 = jnp.float32
BF16 = jnp.bfloat16
HI = lax.Precision.HIGHEST
PARAMS = pltpu.CompilerParams(vmem_limit_bytes=32 * 1024 * 1024)

LIGHT = pl.CostEstimate(flops=0, bytes_accessed=0, transcendentals=0)


def iota(shape, dim):
    return lax.broadcasted_iota(jnp.int32, shape, dim)


def split(x):
    high = x.astype(BF16)
    return high, (x - high.astype(F32)).astype(BF16)


def dot3(a, b_high, b_low):
    a_high, a_low = split(a)
    dot = functools.partial(jnp.dot, preferred_element_type=F32)
    return dot(a_high, b_high) + (dot(a_high, b_low) + dot(a_low, b_high))


def pack_kernel(width, win_ref, out_ref):
    fold = LANES // width
    part = win_ref.shape[0] // fold
    tile = win_ref[:, 0, :]
    lane = iota((part, LANES), 1) // width
    out = tile[:part]
    for j in range(1, fold):
        rolled = pltpu.roll(tile[j * part : (j + 1) * part], j * width, 1)
        out = jnp.where(lane == j, rolled, out)
    out_ref[...] = out


def pack_rows(window, first, rows, tile, width):
    fold = LANES // width
    base = first // tile
    return pl.pallas_call(
        functools.partial(pack_kernel, width),
        grid=(rows // tile,),
        in_specs=[pl.BlockSpec((None, tile, 1, LANES), lambda i: (0, base + i, 0, 0))],
        out_specs=pl.BlockSpec((tile // fold, LANES), lambda i: (i, 0)),
        out_shape=jax.ShapeDtypeStruct((rows // fold, LANES), F32),
        compiler_params=PARAMS,
        cost_estimate=LIGHT,
        name="pack",
    )(window)


def unpack(slots, width):
    fold = LANES // width
    part = slots[0].shape[0]
    lane = iota((part, LANES), 1) // width
    rows = []
    for j in range(fold):
        pieces = []
        for v in range(len(slots) // fold):
            piece = None
            for m in range(fold):
                slot = slots[v * fold + m]
                shift = (m - j) % fold
                moved = pltpu.roll(slot, shift * width, 1) if shift else slot
                piece = moved if piece is None else jnp.where(lane == m, moved, piece)
            pieces.append(piece)
        rows.append(jnp.concatenate(pieces, 1))
    return jnp.concatenate(rows, 0)


def slot_place(count, width, col_index):
    a = iota((KW, KW), 0)
    c = iota((KW, KW), 1)
    source = lax.rem(col_index - a // width + count, count)
    return (c == lax.rem(a, width) * count + source).astype(F32)


def interleave(ref, first, step, rows):
    for v in range(ref.shape[0]):
        piece = rows[:, v * LANES : (v + 1) * LANES]
        ref[v, pl.ds(first, rows.shape[0], stride=step), :] = piece


def whole_rows(ref):
    return jnp.concatenate([ref[v] for v in range(ref.shape[0])], 1)


def eliminate(z_ref, lt_ref):
    rows = iota((BLOCK, 1), 0)
    for b in range(KW // BLOCK):
        top = b * BLOCK
        strip = z_ref[top : top + BLOCK, :]
        scale = jnp.zeros((BLOCK, 1), F32)
        for j in range(BLOCK):
            col = strip[:, top + j : top + j + 1]
            row = strip[j : j + 1, :]
            pivot = strip[j : j + 1, top + j : top + j + 1]
            ratio = jnp.where(rows > j, col / pivot, 0.0)
            scale = jnp.where(rows == j, lax.rsqrt(pivot), scale)
            strip = strip - ratio * row
        strip = strip * scale
        z_ref[top : top + BLOCK, :] = strip
        lt_ref[top : top + BLOCK, :] = strip[:, :KW]
        if top + BLOCK < KW:
            update = lax.dot_general(
                strip[:, :KW], strip, (((0,), (0,)), ((), ())), precision=HI,
                preferred_element_type=F32,
            )
            z_ref[top + BLOCK :, :] = z_ref[top + BLOCK :, :] - update[top + BLOCK :, :]


def factor_kernel(
    count, width, place_ref, s_ref, high_ref, low_ref, diag_ref, z_ref, lt_ref, mix_ref
):
    row_count, height = s_ref.shape[0], s_ref.shape[1]
    for p in range(row_count):
        interleave(mix_ref, p, row_count, s_ref[p])
    place = slot_place(count, width, place_ref[1])
    s = jnp.dot(whole_rows(mix_ref), place, precision=HI, preferred_element_type=F32)
    r = iota((KW, KW), 0)
    c = iota((KW, KW), 1)
    z_ref[:, :KW] = jnp.where(r >= c, s, 0.0) + jnp.where(r > c, s, 0.0).T
    z_ref[:, KW:] = (r == c).astype(F32)
    eliminate(z_ref, lt_ref)
    contract_last = (((1,), (1,)), ((), ()))
    inverse = jnp.where(r >= c, z_ref[:, KW:], 0.0)
    weights = lax.dot_general(
        place, inverse, contract_last, precision=HI, preferred_element_type=F32
    )
    high_ref[...], low_ref[...] = split(weights)
    upper = jnp.where(r <= c, lt_ref[...], 0.0)
    pick = iota((height, KW), 1) == iota((height, KW), 0) * row_count + place_ref[0]
    diag_ref[...] = lax.dot_general(
        pick.astype(F32), upper, contract_last, precision=HI, preferred_element_type=F32
    )


def whole(*shape):
    return pl.BlockSpec(shape, lambda i, place: (0,) * len(shape))


def factor_call(place, gathered, count, width):
    row_count, height = gathered.shape[0], gathered.shape[1]
    return pl.pallas_call(
        functools.partial(factor_kernel, count, width),
        grid_spec=pltpu.PrefetchScalarGridSpec(
            num_scalar_prefetch=1,
            grid=(1,),
            in_specs=[whole(row_count, height, KW)],
            out_specs=[whole(KW, KW), whole(KW, KW), whole(height, KW)],
            scratch_shapes=[
                pltpu.VMEM((KW, 2 * KW), F32),
                pltpu.VMEM((KW, KW), F32),
                pltpu.VMEM((KW // LANES, KW, LANES), F32),
            ],
        ),
        out_shape=[
            jax.ShapeDtypeStruct((KW, KW), BF16),
            jax.ShapeDtypeStruct((KW, KW), BF16),
            jax.ShapeDtypeStruct((height, KW), F32),
        ],
        compiler_params=PARAMS,
        cost_estimate=LIGHT,
        name="factor",
    )(place, gathered)


def columns_kernel(count, width, place_ref, head_ref, nh_ref, nl_ref, high_ref, low_ref, scr_ref):
    groups = head_ref.shape[0]
    tiles = head_ref.shape[2]
    height = head_ref.shape[3] * (LANES // width)
    for a in range(groups):
        for t in range(tiles):
            raw = unpack([head_ref[a, s, t] for s in range(count)], width)
            panel = dot3(raw, nh_ref[...], nl_ref[...])
            interleave(scr_ref, t * height * groups + a, groups, panel)
    cols = scr_ref.shape[1]
    l = iota((cols, KW), 0)
    c = iota((cols, KW), 1)
    pick = jnp.where(c == l * count + place_ref[1], -1.0, 0.0)
    weights = jnp.where(l < width, pick, whole_rows(scr_ref)).T
    high_ref[...], low_ref[...] = split(weights)


def columns_call(place, head, n_high, n_low, count, width, cols):
    return pl.pallas_call(
        functools.partial(columns_kernel, count, width),
        grid_spec=pltpu.PrefetchScalarGridSpec(
            num_scalar_prefetch=1,
            grid=(1,),
            in_specs=[whole(*head.shape), whole(KW, KW), whole(KW, KW)],
            out_specs=[whole(KW, cols), whole(KW, cols)],
            scratch_shapes=[pltpu.VMEM((KW // LANES, cols, LANES), F32)],
        ),
        out_shape=[jax.ShapeDtypeStruct((KW, cols), BF16)] * 2,
        compiler_params=PARAMS,
        cost_estimate=LIGHT,
        name="columns",
    )(place, head, n_high, n_low)


def update_kernel(count, width, row_count, first, skip, rows, tile, place_ref, *refs):
    ins = len(refs) - 10 - (first > 0)
    slots_in = refs[:ins]
    nh_ref, nl_ref, wh_ref, wl_ref, diag_ref, win_ref = refs[ins : ins + 6]
    out_ref, ring_ref, in_sem, out_sem = refs[-4:]
    p, q = place_ref[0], place_ref[1]
    groups = wh_ref.shape[1] // LANES
    part = tile // (LANES // width)
    steps = rows // tile
    depth = ring_ref.shape[0]
    ahead = steps if steps <= depth else depth // 2
    height = tile * groups
    dot = functools.partial(jnp.dot, preferred_element_type=F32)

    def place_of(i):
        return pl.ds(pl.multiple_of(first * groups + i * height, height), height)

    def fetch(i):
        slot = lax.rem(i, depth)
        return pltpu.make_async_copy(win_ref.at[place_of(i), :], ring_ref.at[slot], in_sem.at[slot])

    def store(i):
        slot = lax.rem(i, depth)
        return pltpu.make_async_copy(ring_ref.at[slot], out_ref.at[place_of(i), :], out_sem.at[slot])

    for i in range(ahead):
        fetch(jnp.int32(i)).start()

    def step(i, carry):
        span = pl.ds(pl.multiple_of(skip // (LANES // width) + i * part, part), part)
        slots = [slots_in[s][span, :] for s in range(count)]
        if ins > count:
            forwarded = slots_in[count][span, :]
            slots[1] = jnp.where(q == 0, forwarded, slots[1])
            slots[count - 1] = jnp.where(q == count - 1, forwarded, slots[count - 1])
        panel = dot3(unpack(slots, width), nh_ref[...], nl_ref[...])
        lane = iota((tile, LANES), 1)
        if first == 0:
            tall = diag_ref.shape[0]
            top = jnp.where(i == 0, diag_ref[...], panel[:tall])
            panel = jnp.concatenate([top, panel[tall:]], 0)
            global_row = (iota((tile, LANES), 0) + i * tile) * row_count + p
        high, low = split(panel)
        fetch(i).wait()
        buf = ring_ref.at[lax.rem(i, depth)]
        for pair in range(groups // 2):
            cols = slice(pair * 2 * LANES, (pair + 1) * 2 * LANES)
            w_high, w_low = wh_ref[:, cols], wl_ref[:, cols]
            update = dot(high, w_high) + (dot(high, w_low) + dot(low, w_high))
            for half in range(2):
                g = pair * 2 + half
                old = buf[pl.ds(g, tile, stride=groups), :]
                if g * LANES < width:
                    old = jnp.where(lane < width - g * LANES, 0.0, old)
                new = old - update[:, half * LANES : (half + 1) * LANES]
                if first == 0:
                    global_col = (lane + g * LANES) * count + q
                    new = jnp.where(global_row >= global_col, new, 0.0)
                buf[pl.ds(g, tile, stride=groups), :] = new
        store(i).start()

        @pl.when(i + ahead < steps)
        def _():
            @pl.when(i + ahead >= depth)
            def _():
                store(i + ahead - depth).wait()

            fetch(i + ahead).start()

        return carry

    lax.fori_loop(0, steps, step, 0)

    def drain(i, carry):
        store(i).wait()
        return carry

    lax.fori_loop(max(0, steps - depth), steps, drain, 0)


def update_call(
    place, chunk, weights, flat, out, first, skip, rows, tile, count, width, row_count
):
    groups = weights[2].shape[1] // LANES
    held = pl.BlockSpec(memory_space=pltpu.VMEM)
    far = pl.BlockSpec(memory_space=pl.ANY)
    specs = [held] * (len(chunk) + len(weights)) + [far]
    operands = [*chunk, *weights, flat]
    aliases = {}
    if out is not None:
        specs.append(far)
        operands.append(out)
        aliases = {len(operands): 0}
    depth = min(DEPTH, rows // tile)
    return pl.pallas_call(
        functools.partial(update_kernel, count, width, row_count, first, skip, rows, tile),
        grid_spec=pltpu.PrefetchScalarGridSpec(
            num_scalar_prefetch=1,
            grid=(1,),
            in_specs=specs,
            out_specs=far,
            scratch_shapes=[
                pltpu.VMEM((depth, tile * groups, LANES), F32),
                pltpu.SemaphoreType.DMA((depth,)),
                pltpu.SemaphoreType.DMA((depth,)),
            ],
        ),
        out_shape=jax.ShapeDtypeStruct(flat.shape, F32),
        input_output_aliases=aliases,
        compiler_params=PARAMS,
        cost_estimate=pl.CostEstimate(
            flops=6 * rows * KW * (KW + groups * LANES),
            bytes_accessed=rows * 4 * (2 * groups * LANES + KW),
            transcendentals=0,
        ),
        name="update",
    )(place, *operands)


def chunk_sizes(units):
    sizes = [1]
    for share in SHARES:
        sizes.append(max(1, units * share // 16))
    return sizes + [units - sum(sizes)]


def body(window):
    local_rows = window.shape[1]
    local_cols = window.shape[3]
    row_count = lax.axis_size("row")
    count = lax.axis_size("col")
    p = lax.axis_index("row")
    q = lax.axis_index("col")
    width = KW // count
    height = KW // row_count
    head_rows = local_cols * count // row_count
    groups = row_count // count
    tile = min(TILE, head_rows)
    place = jnp.stack([p, q]).astype(jnp.int32)
    flat = window.reshape(local_rows * local_cols // LANES, LANES)

    sizes = [x * tile for x in chunk_sizes(local_rows // tile)]
    starts = [sum(sizes[:i]) for i in range(len(sizes))]
    packed = [pack_rows(window, f, r, tile, width) for f, r in zip(starts, sizes)]

    def shift(x, k):
        return lax.ppermute(x, "col", [(i, (i + k) % count) for i in range(count)])

    fold = LANES // width
    slots = [[packed[0]] + [shift(packed[0], k) for k in range(1, count)]]
    early = tuple(packed[1:3])
    slots[0] = list(lax.optimization_barrier((*slots[0], *early)))[:count]
    head = jnp.stack(slots[0])

    lead = head[:, :height, :width]
    lead = lead.transpose(1, 0, 2).reshape(height, KW)
    gathered = lax.all_gather(lead, "row")
    n_high, n_low, diag = factor_call(place, gathered, count, width)

    spread = head
    bit = 1
    while bit < count:
        pairs = [(i, i ^ bit) for i in range(row_count)]
        other = lax.ppermute(spread, "row", pairs)
        spread = jnp.where(((p ^ q) & bit) != 0, other, spread)
        bit *= 2
    spread = spread[None]
    while bit < row_count:
        pairs = [(i, i ^ bit) for i in range(row_count)]
        other = lax.ppermute(spread, "row", pairs)
        low = (p & bit) == 0
        spread = jnp.concatenate(
            [jnp.where(low, spread, other), jnp.where(low, other, spread)], 0
        )
        bit *= 2
    spread = spread.reshape(groups, count, head_rows // tile, tile // fold, LANES)

    def update(j, out, skip=0, rows=None):
        rows = sizes[j] - skip if rows is None else rows
        return update_call(
            place, slots[j], weights, flat, out, starts[j] + skip, skip, rows, tile,
            count, width, row_count,
        )

    after = lambda x, *others: lax.optimization_barrier((x, *others))[0]

    if count != 4:
        slots += [[x] + [shift(x, k) for k in range(1, count)] for x in packed[1:]]
        made = columns_call(place, spread, n_high, n_low, count, width, local_cols)
        weights = [n_high, n_low, *made, diag]
        out = None
        for j in range(len(sizes)):
            out = update(j, out)
        return out.reshape(window.shape)

    up = [(0, 1), (1, 2), (2, 3)]
    down = [(1, 0), (2, 1), (3, 2)]
    outward = [(2, 3), (1, 0)]
    send = lambda x, pairs: lax.ppermute(x, "col", pairs)

    def forward(j, *others):
        slots[j].append(send(after(slots[j][2], *others), outward))

    x = packed[1]
    slots.append([x, send(x, up), shift(x, 2), send(x, down)])
    forward(1, n_high)
    made = columns_call(place, spread, n_high, n_low, count, width, local_cols)
    weights = [n_high, n_low, *made, diag]
    out = update(0, None)
    x, third, slots[1][1], slots[1][3] = lax.optimization_barrier(
        (packed[2], packed[3], slots[1][1], slots[1][3])
    )
    slots.append([x, send(x, up), shift(x, 2), send(x, down)])
    part = -(-sizes[1] // tile // 2) * tile
    out = update(1, out, rows=part)
    slots[2][2], third, out = lax.optimization_barrier((slots[2][2], third, out))
    forward(2)
    slots.append([third, send(third, up), shift(third, 2), send(third, down)])
    out = update(1, out, skip=part)
    slots[3][2], out = lax.optimization_barrier((slots[3][2], out))
    forward(3)
    out = update(2, out)
    out = update(3, out)
    return out.reshape(window.shape)


def solution(mesh):
    spec = P("row", None, "col", None)
    return jax.shard_map(body, mesh=mesh, in_specs=(spec,), out_specs=spec, check_vma=False)
```
